32 devices in a mesh: groups: 2 (over y), tile: 4 (over z), plane: 2 (over x), inst: 2 (over core).
Axes of the slice: x: 2, y: 2, z: 4, core: 2. Of those that a mesh axis runs over, the one named last changes fastest.
Arguments:
- state: float32 [48, 10, 2, 32, 128], P('inst', 'groups', 'plane', 'tile'), parts along dimension 1, may hold values from -6 to 6
- boundary: float32 [48, 2, 10, 32, 128], P('inst', None, 'groups', ('tile', 'plane')), parts along dimension 2, may hold values from -6 to 6
- inv_volume: float32 [4, 32, 128], P(('groups', 'plane'), 'tile'), parts along dimension 0, may hold values from 0.5 to 2
- flux_matrix: float32 [6, 5, 5], P('groups'), parts along dimension 0, may hold values from -2.5 to 2.5
- left_vectors: float32 [10, 5], P('groups'), parts along dimension 0, may hold values from -2.5 to 2.5
- right_vectors: float32 [10, 5], P('groups'), parts along dimension 0, may hold values from -2.5 to 2.5
- gain: float32 [4, 2, 64, 2, 3], P('groups'), parts along dimension 0, may hold values from -3 to 3
- harmonic_index: int32 [40], P('groups'), parts along dimension 0, may hold values from 1 to 23, as said below
- mode_count: int32 [4, 128], P('groups'), parts along dimension 0, may hold values from 1 to 64
Outputs:
- residual: float32 [48, 10, 2, 32, 128], P('inst', 'groups', 'plane', 'tile'), parts along dimension 1
- corrected: float32 [48, 2, 10, 32, 128], P('inst', None, 'groups', ('tile', 'plane')), parts along dimension 2
The draws below stay inside these ranges and needn't reach their ends.
There are 2 independent parts, one for each index of `groups`. The reference program is written for one: setup_inputs(seed, part) draws one part's arguments, and reference() takes and returns one part's arrays. A program takes and returns all parts, laid end to end along the dimension named above; each array names one. Nothing has to cross between parts.
Inputs may be any that keep to these rules, and one draw needn't show every extreme that they name: `harmonic_index`: 20 distinct values in rising order; the first is 1 and the last is 23.
All inputs are finite; a program needn't handle non-finite values.
Results may differ from the reference program's by a relative error of at most 0.0001.
Values sent between devices are 32-bit elements; how exact they have to be, the bound alone decides.
A program may use at most 64 MiB of HBM per device.

```python
import math
import jax
import jax.numpy as jnp
from jax import lax

NV = 5
NI = 2
NO = 3
NT = 48
KH = 20
MODES = 64
NR = 128
NC = 32
NA = 2


def draw_harmonic_index(key, part):
    middle = jax.random.permutation(jax.random.fold_in(key, 11), NT // 2 - 3).astype(jnp.int32) + 2
    chosen = middle[:KH - 2]
    ends = jnp.array([1, NT // 2 - 1], dtype=jnp.int32)
    return jnp.sort(jnp.concatenate([ends, chosen]))


def with_ends(values, rng, low, top_value):
    dims = values.shape
    place = [jax.random.randint(jax.random.fold_in(rng, axis), (), 0, dims[axis]) for axis in range(len(dims))]
    values = values.at[tuple(place)].set(low)
    longest = dims.index(max(dims))
    place[longest] = (place[longest] + 1) % dims[longest]
    return values.at[tuple(place)].set(top_value)


def level_of(rng, dims, split, smallest, largest):
    level, own = 1.0, jax.random.fold_in(rng, 6)
    for dim, parts in split:
        heights = jnp.exp(jax.random.uniform(jax.random.fold_in(own, dim), (parts,), jnp.float32, smallest / len(split), largest / len(split)))
        level = level * jnp.repeat(heights, dims[dim] // parts).reshape([-1 if axis == dim else 1 for axis in range(len(dims))])
    return level


def scatter_about(rng, shape, spread, limit, cuts=(), kind=jnp.bfloat16):
    entries = spread * jax.random.normal(rng, shape, jnp.float32)
    if cuts:
        entries = entries * level_of(rng, shape, cuts, -0.22, 0.18)
    return jnp.clip(entries, -limit, limit).astype(kind)


def setup_inputs(seed: int = 0, part: int = 0) -> dict:
    arg_keys = jax.random.split(jax.random.key(seed), 10)
    part_splits = jax.random.split(jax.random.fold_in(arg_keys[9], part), 10)
    return {
        "state": scatter_about(part_splits[0], (NT, NV, NA, NC, NR), 1.0, 6.0, ((0, 2), (2, 2), (3, 4)), jnp.float32),
        "boundary": scatter_about(part_splits[1], (NT, 2, NV, NC, NR), 1.0, 6.0, ((0, 2), (3, 8)), jnp.float32),
        "inv_volume": jnp.clip(jnp.exp(math.log(2.0) - 1.3862944 * jax.random.uniform(part_splits[2], (NA, NC, NR), jnp.float32) ** level_of(part_splits[2], (NA, NC, NR), ((0, 2), (1, 4)), -0.2, 0.2)), 0.5, 2.0),
        "flux_matrix": scatter_about(part_splits[3], (3, NV, NV), NV ** -0.5, 2.5, (), jnp.float32),
        "left_vectors": scatter_about(part_splits[4], (NV, NV), NV ** -0.5, 2.5, (), jnp.float32),
        "right_vectors": scatter_about(part_splits[5], (NV, NV), NV ** -0.5, 2.5, (), jnp.float32),
        "gain": scatter_about(part_splits[6], (2, 2, MODES, NI, NO), 0.5, 3.0, (), jnp.float32),
        "harmonic_index": draw_harmonic_index(jax.random.fold_in(jax.random.fold_in(arg_keys[9], part), 71), part),
        "mode_count": with_ends(jax.random.randint(part_splits[8], (2, NR), 1, MODES + 1), jax.random.fold_in(part_splits[8], 1), 1, MODES).astype(jnp.int32),
    }


precise = lax.Precision.HIGHEST
DISSIPATION = 0.25
OMEGA_SCALE = 0.1


def cell_tables(cell_ids, mode_total, period):
    product = (cell_ids[:, None] * jnp.arange(mode_total, dtype=jnp.int32)[None, :]) % period
    phases = product.astype(jnp.float32) * (2.0 * math.pi / period)
    return jnp.cos(phases), jnp.sin(phases)


def time_tables(harmonic_index, instance_ids, period):
    product = (instance_ids[:, None] * harmonic_index[None, :]) % period
    phases = product.astype(jnp.float32) * (2.0 * math.pi / period)
    cos_table = jnp.cos(phases)
    sin_table = jnp.sin(phases)
    frequency = harmonic_index.astype(jnp.float32)[None, :]
    analysis = jnp.concatenate([cos_table, sin_table], axis=1).T * (2.0 / period)
    synthesis = jnp.concatenate([-frequency * sin_table, frequency * cos_table], axis=1) * OMEGA_SCALE
    return analysis, synthesis


def giles_planes(boundary, left_vectors, right_vectors, gain, mode_count):
    cos_table, sin_table = cell_tables(jnp.arange(NC, dtype=jnp.int32), MODES, NC)
    weight = 2.0 / NC
    hat_cos = jnp.einsum("tpvcr,cm->tpvmr", boundary, cos_table * weight, precision=precise)
    hat_sin = jnp.einsum("tpvcr,cm->tpvmr", boundary, sin_table * weight, precision=precise)
    wave_cos = jnp.einsum("uv,tpvmr->tpumr", left_vectors, hat_cos, precision=precise)
    wave_sin = jnp.einsum("uv,tpvmr->tpumr", left_vectors, hat_sin, precision=precise)
    gain_real = gain[:, 0]
    gain_imag = gain[:, 1]
    out_cos = wave_cos[:, :, NI:]
    out_sin = wave_sin[:, :, NI:]
    target_cos = jnp.einsum("pmio,tpomr->tpimr", gain_real, out_cos, precision=precise) - jnp.einsum("pmio,tpomr->tpimr", gain_imag, out_sin, precision=precise)
    target_sin = jnp.einsum("pmio,tpomr->tpimr", gain_imag, out_cos, precision=precise) + jnp.einsum("pmio,tpomr->tpimr", gain_real, out_sin, precision=precise)
    resolved = (jnp.arange(MODES, dtype=jnp.int32)[None, :, None] < mode_count[:, None, :]).astype(jnp.float32)
    jump_cos = (target_cos - wave_cos[:, :, :NI]) * resolved[None, :, None]
    jump_sin = (target_sin - wave_sin[:, :, :NI]) * resolved[None, :, None]
    back_cos = jnp.einsum("ui,tpimr->tpumr", right_vectors[:, :NI], jump_cos, precision=precise)
    back_sin = jnp.einsum("ui,tpimr->tpumr", right_vectors[:, :NI], jump_sin, precision=precise)
    delta = jnp.einsum("tpumr,cm->tpucr", back_cos, cos_table, precision=precise) + jnp.einsum("tpumr,cm->tpucr", back_sin, sin_table, precision=precise)
    return boundary + delta


def reference(state, boundary, inv_volume, flux_matrix, left_vectors, right_vectors, gain, harmonic_index, mode_count):
    corrected = giles_planes(boundary, left_vectors, right_vectors, gain, mode_count)

    def flux_one(inputs):
        field, inlet_layer, exit_layer = inputs
        axial = jnp.concatenate([inlet_layer[:, None], field, exit_layer[:, None]], axis=1)
        radial = jnp.pad(field, ((0, 0), (0, 0), (0, 0), (1, 1)))
        neighbours = ((axial[:, 2:], axial[:, :-2]), (jnp.roll(field, -1, axis=2), jnp.roll(field, 1, axis=2)), (radial[..., 2:], radial[..., :-2]))
        total = jnp.zeros_like(field)
        for direction in range(3):
            forward, backward = neighbours[direction]
            total = total + jnp.einsum("vw,wacr->vacr", flux_matrix[direction], 0.5 * (forward - backward), precision=precise)
            total = total - DISSIPATION * (forward - 2.0 * field + backward)
        return inv_volume[None] * total

    flux = lax.map(flux_one, (state, corrected[:, 0], corrected[:, 1]))
    analysis, synthesis = time_tables(harmonic_index, jnp.arange(NT, dtype=jnp.int32), NT)
    flat_state = state.reshape(NT, -1)
    coefficients = jnp.dot(analysis, flat_state, precision=precise)
    rate = jnp.dot(synthesis, coefficients, precision=precise).reshape(state.shape)
    return flux + rate, corrected
```

```python
import functools
import math

import jax
import jax.numpy as jnp
import numpy as np
from jax import lax
from jax.experimental import pallas as pl
from jax.experimental.pallas import tpu as pltpu
from jax.sharding import PartitionSpec as P

NI = 2


precise = lax.Precision.HIGHEST
DISSIPATION = 0.25
OMEGA_SCALE = 0.1


def padded_2(x, sides, width):
    for axis, dim in sides:
        size, length = (lax.axis_size(axis), x.shape[dim])
        up = [(i, (i + 1) % size) for i in range(size)]
        down = [(j, i) for i, j in up]
        last = lax.slice_in_dim(x, length - width, length, axis=dim)
        initial = lax.slice_in_dim(x, 0, width, axis=dim)
        before = lax.ppermute(last, axis, up)
        after = lax.ppermute(initial, axis, down)
        x = jnp.concatenate([before, x, after], axis=dim)
    return x


def cell_tables(cell_ids, mode_total, period):
    product = cell_ids[:, None] * jnp.arange(mode_total, dtype=jnp.int32)[None, :] % period
    phases = product.astype(jnp.float32) * (2.0 * math.pi / period)
    return (jnp.cos(phases), jnp.sin(phases))


def time_tables(harmonic_index, instance_ids, period):
    product = instance_ids[:, None] * harmonic_index[None, :] % period
    phases = product.astype(jnp.float32) * (2.0 * math.pi / period)
    cos_table = jnp.cos(phases)
    sin_table = jnp.sin(phases)
    frequency = harmonic_index.astype(jnp.float32)[None, :]
    analysis = jnp.concatenate([cos_table, sin_table], axis=1).T * (2.0 / period)
    synthesis = (
        jnp.concatenate([-frequency * sin_table, frequency * cos_table], axis=1) * OMEGA_SCALE
    )
    return (analysis, synthesis)


def correct_block(block, cell_ids, period, left_vectors, right_vectors, gain, resolved):
    mode_total = gain.shape[2]
    cos_table, sin_table = cell_tables(cell_ids, mode_total, period)
    both_tables = jnp.concatenate([cos_table, sin_table], axis=1)
    spectrum = jnp.einsum("tpvcr,cm->tpvmr", block, both_tables * (2.0 / period), precision=precise)
    hat_cos = spectrum[:, :, :, :mode_total]
    hat_sin = spectrum[:, :, :, mode_total:]
    wave_cos = jnp.einsum("uv,tpvmr->tpumr", left_vectors, hat_cos, precision=precise)
    wave_sin = jnp.einsum("uv,tpvmr->tpumr", left_vectors, hat_sin, precision=precise)
    gain_real = gain[:, 0]
    gain_imag = gain[:, 1]
    out_cos = wave_cos[:, :, NI:]
    out_sin = wave_sin[:, :, NI:]
    target_cos = jnp.einsum(
        "pmio,tpomr->tpimr", gain_real, out_cos, precision=precise
    ) - jnp.einsum("pmio,tpomr->tpimr", gain_imag, out_sin, precision=precise)
    target_sin = jnp.einsum(
        "pmio,tpomr->tpimr", gain_imag, out_cos, precision=precise
    ) + jnp.einsum("pmio,tpomr->tpimr", gain_real, out_sin, precision=precise)
    jump_cos = (target_cos - wave_cos[:, :, :NI]) * resolved[None, :, None]
    jump_sin = (target_sin - wave_sin[:, :, :NI]) * resolved[None, :, None]
    back_cos = jnp.einsum("ui,tpimr->tpumr", right_vectors[:, :NI], jump_cos, precision=precise)
    back_sin = jnp.einsum("ui,tpimr->tpumr", right_vectors[:, :NI], jump_sin, precision=precise)
    joined = jnp.concatenate([back_cos, back_sin], axis=3)
    delta = jnp.einsum("tpumr,cm->tpucr", joined, both_tables, precision=precise)
    return block + delta


def local(
    state,
    boundary,
    inv_volume,
    flux_matrix,
    left_vectors,
    right_vectors,
    gain,
    harmonic_index,
    mode_count,
):
    tiles = lax.axis_size("tile")
    planes = lax.axis_size("plane")
    face_cells = boundary.shape[3]
    period = face_cells * tiles * planes
    local_stations = boundary.shape[4] // (tiles * planes)
    station = lax.axis_index("tile") * planes + lax.axis_index("plane")
    station_modes = lax.dynamic_slice_in_dim(
        mode_count, station * local_stations, local_stations, 1
    )
    resolved = (
        jnp.arange(gain.shape[2], dtype=jnp.int32)[None, :, None] < station_modes[:, None, :]
    ).astype(jnp.float32)
    natural_ids = jnp.arange(period, dtype=jnp.int32)
    fixed = correct_block(
        lax.all_to_all(boundary, ("tile", "plane"), split_axis=4, concat_axis=3, tiled=True),
        natural_ids,
        period,
        left_vectors,
        right_vectors,
        gain,
        resolved,
    )
    corrected = lax.all_to_all(fixed, ("tile", "plane"), split_axis=3, concat_axis=4, tiled=True)
    padded = padded_2(state, (("tile", 3), ("plane", 2)), 1)
    layers = lax.all_gather(corrected, "plane", axis=3, tiled=True)
    plane_pos = lax.axis_index("plane")
    centre = padded[:, :, :, 1:-1]
    inlet_layer = jnp.where(plane_pos == 0, layers[:, 0], centre[:, :, 0])
    exit_layer = jnp.where(plane_pos == planes - 1, layers[:, 1], centre[:, :, -1])
    axial = jnp.concatenate([inlet_layer[:, :, None], state, exit_layer[:, :, None]], axis=2)
    radial = jnp.pad(state, ((0, 0), (0, 0), (0, 0), (0, 0), (1, 1)))
    middle = padded[:, :, 1:-1]
    neighbours = (
        (axial[:, :, 2:], axial[:, :, :-2]),
        (middle[:, :, :, 2:], middle[:, :, :, :-2]),
        (radial[..., 2:], radial[..., :-2]),
    )
    total = jnp.zeros_like(state)
    for direction in range(3):
        forward, backward = neighbours[direction]
        total = total + jnp.einsum(
            "vw,twacr->tvacr", flux_matrix[direction], 0.5 * (forward - backward), precision=precise
        )
        total = total - DISSIPATION * (forward - 2.0 * state + backward)
    flux = inv_volume[None, None] * total
    local_count = state.shape[0]
    total_count = local_count * lax.axis_size("inst")
    instance_ids = lax.axis_index("inst") * local_count + jnp.arange(local_count, dtype=jnp.int32)
    analysis_local, synthesis_local = time_tables(harmonic_index, instance_ids, total_count)
    flat_state = state.reshape(local_count, -1)
    analysis_full, unused_table = time_tables(
        harmonic_index, jnp.arange(total_count, dtype=jnp.int32), total_count
    )
    combined = jnp.dot(synthesis_local, analysis_full, precision=precise)
    rate = jnp.dot(
        combined, lax.all_gather(flat_state, "inst", axis=0, tiled=True), precision=precise
    )
    residual = flux + rate.reshape(state.shape)
    return (residual, corrected)


def fast_kernel(
    sizes,
    state,
    boundary,
    volume,
    flux_m,
    left_m,
    right_m,
    columns,
    counts,
    taps,
    analysis,
    synthesis,
    residual,
    corrected,
    own,
    twin,
    beside,
    faces,
    halves,
    spread,
    out8,
    out4,
    in8,
    in4,
    edges,
    below,
    above,
    taps_wide,
    gains,
    resolved,
    local_sem,
    swap_send,
    swap_recv,
    spread_send,
    spread_recv,
    back_send,
    back_recv,
    state_send,
    state_recv,
):
    tiles, steps, variables, cells, face_cells, modes, period = sizes
    share = steps // tiles
    tile = lax.axis_index("tile")
    plane = lax.axis_index("plane")
    inst = lax.axis_index("inst")
    other = 1 - plane
    mesh_id = pl.DeviceIdType.MESH
    others = [lax.rem(tile + j, tiles) for j in range(tiles)]

    own_copy = pltpu.make_async_copy(state, own, local_sem.at[0])
    own_copy.start()
    face_copy = pltpu.make_async_copy(boundary, faces, local_sem.at[1])
    face_copy.start()
    half_copy = pltpu.make_async_copy(boundary.at[:, plane], halves.at[plane], local_sem.at[2])
    half_copy.start()

    barrier = pltpu.get_barrier_semaphore()
    for j in range(tiles):
        if j:
            pl.semaphore_signal(
                barrier, inc=1, device_id={"tile": others[j]}, device_id_type=mesh_id
            )
        pl.semaphore_signal(
            barrier,
            inc=1,
            device_id={"tile": others[j], "plane": other},
            device_id_type=mesh_id,
        )
    pl.semaphore_signal(barrier, inc=1, device_id={"inst": 1 - inst}, device_id_type=mesh_id)
    pl.semaphore_wait(barrier, 2 * tiles)

    def remote(src, dst, send, recv, where):
        return pltpu.make_async_remote_copy(
            src_ref=src,
            dst_ref=dst,
            send_sem=send,
            recv_sem=recv,
            device_id=where,
            device_id_type=mesh_id,
        )

    def part(k):
        return pl.ds(k * share, share)

    swaps = []
    for j in [*range(1, tiles), 0]:
        swap = remote(
            boundary.at[part(others[j]), other],
            halves.at[plane, part(others[j])],
            swap_send.at[j],
            swap_recv.at[j],
            {"plane": other},
        )
        swap.start()
        swaps.append((j, swap))
    sent = []
    for j in range(1, tiles):
        copy = remote(
            boundary.at[part(others[j]), plane],
            spread.at[tile, plane],
            spread_send.at[j, 0],
            spread_recv.at[tile, plane],
            {"tile": others[j]},
        )
        copy.start()
        sent.append(copy)
    twin_copy = remote(state, twin, state_send.at[0], state_recv.at[0], {"inst": 1 - inst})
    twin_copy.start()
    home = pltpu.make_async_copy(
        boundary.at[part(tile), plane], spread.at[tile, plane], local_sem.at[3]
    )
    home.start()

    own_copy.wait()

    @pl.loop(0, steps)
    def _(t):
        for v in range(variables):
            edges[0, v, pl.ds(t, 1), :] = own[t, v, cells - 1 : cells, :]
            edges[1, v, pl.ds(t, 1), :] = own[t, v, 0:1, :]

    up = remote(
        edges.at[0], below, state_send.at[1], state_recv.at[1], {"tile": others[1]}
    )
    up.start()
    down = remote(
        edges.at[1], above, state_send.at[2], state_recv.at[2], {"tile": others[tiles - 1]}
    )
    down.start()

    for j, swap in swaps:
        swap.wait_recv()
        if j:
            copy = remote(
                halves.at[other, part(others[j])],
                spread.at[tile, other],
                spread_send.at[j, 1],
                spread_recv.at[tile, other],
                {"tile": others[j]},
            )
            copy.start()
            sent.append(copy)
    away = pltpu.make_async_copy(
        halves.at[other, part(tile)], spread.at[tile, other], local_sem.at[4]
    )
    away.start()
    beside_copy = remote(state, beside, state_send.at[3], state_recv.at[3], {"plane": other})
    beside_copy.start()

    count_row = jnp.where(plane == 0, counts[0:1, :], counts[1:2, :])
    stations = counts.shape[1]
    mode_row = lax.broadcasted_iota(jnp.int32, (period, stations), 0)
    mask = [
        (mode_row + a * period < count_row).astype(jnp.float32) for a in range(modes // period)
    ]
    resolved[...] = sum(mask[1:], mask[0])
    for k in range(gains.shape[0]):
        total = None
        for a in range(modes // period):
            column = columns[plane, a * period : (a + 1) * period, k : k + 1]
            term = mask[a] * jnp.broadcast_to(column, (period, stations))
            total = term if total is None else total + term
        gains[k] = total

    @pl.loop(0, 3 * steps)
    def _(e):
        taps_wide[e] = jnp.full((cells, stations), taps[e], jnp.float32)

    twin_copy.wait_recv()

    @pl.loop(0, variables)
    def _(v):
        @pl.loop(0, steps // 8)
        def _(block):
            base = steps - 8 * block
            held = {}

            def tap(offset):
                if offset not in held:
                    held[offset] = taps_wide[base + offset]
                return held[offset]

            sums = [None] * 8
            for source, shift in ((own, 0), (twin, steps)):
                for j in range(steps):
                    x = source[j, v]
                    for i in range(8):
                        term = tap(j - i + shift) * x
                        sums[i] = term if sums[i] is None else sums[i] + term
            for i in range(8):
                residual[8 * block + i, v] = sums[i]

    up.wait_recv()
    down.wait_recv()
    inv_volume = volume[0]
    row = lax.broadcasted_iota(jnp.int32, (cells, stations), 0)
    lane = lax.broadcasted_iota(jnp.int32, (cells, stations), 1)

    @pl.loop(0, steps)
    def _(t):
        around, across, rest = [], [], []
        for v in range(variables):
            s = own[t, v]
            ahead = jnp.where(
                row == cells - 1, above[v, pl.ds(t, 1), :], pltpu.roll(s, cells - 1, 0)
            )
            behind = jnp.where(row == 0, below[v, pl.ds(t, 1), :], pltpu.roll(s, 1, 0))
            outer = jnp.where(lane == stations - 1, 0.0, pltpu.roll(s, stations - 1, 1))
            inner = jnp.where(lane == 0, 0.0, pltpu.roll(s, 1, 1))
            around.append(0.5 * (ahead - behind))
            across.append(0.5 * (outer - inner))
            rest.append(DISSIPATION * (6.0 * s - (ahead + behind + outer + inner)))
        for u in range(variables):
            total = rest[u]
            for w in range(variables):
                total = total + flux_m[1, u, w] * around[w]
                total = total + flux_m[2, u, w] * across[w]
            residual[t, u] = residual[t, u] + inv_volume * total

    home.wait()
    away.wait()
    for j in range(1, tiles):
        for h in range(2):
            remote(
                spread.at[others[j], h],
                spread.at[others[j], h],
                spread_send.at[j, h],
                spread_recv.at[others[j], h],
                {"tile": others[j]},
            ).wait_recv()

    def correct(t):
        x = [
            jnp.concatenate(
                [spread[k, h, t, v] for k in range(tiles) for h in range(2)], axis=0
            )
            for v in range(variables)
        ]
        mixed = []
        for u in range(variables):
            total = left_m[u, 0] * x[0]
            for v in range(1, variables):
                total = total + left_m[u, v] * x[v]
            mixed.append(total)
        waves = jnp.dot(
            analysis[...],
            jnp.concatenate(mixed, axis=1),
            precision=precise,
            preferred_element_type=jnp.float32,
        )
        part_cos = [waves[:period, u * stations : (u + 1) * stations] for u in range(variables)]
        part_sin = [waves[period:, u * stations : (u + 1) * stations] for u in range(variables)]
        jumps = []
        outgoing = variables - NI
        for i in range(NI):
            jump_cos = -resolved[...] * part_cos[i]
            jump_sin = -resolved[...] * part_sin[i]
            for o in range(outgoing):
                real = gains[i * outgoing + o]
                imag = gains[(NI + i) * outgoing + o]
                jump_cos = jump_cos + real * part_cos[NI + o] - imag * part_sin[NI + o]
                jump_sin = jump_sin + imag * part_cos[NI + o] + real * part_sin[NI + o]
            jumps.append(jnp.concatenate([jump_cos, jump_sin], axis=0))
        delta = jnp.dot(
            synthesis[...],
            jnp.concatenate(jumps, axis=1),
            precision=precise,
            preferred_element_type=jnp.float32,
        )
        for k in range(tiles):
            for i in range(NI):
                block = delta[k * cells : (k + 1) * cells, i * stations : (i + 1) * stations]
                out8[k, t, i] = block
                out4[k, t, i] = jnp.where(plane == 0, block[face_cells:], block[:face_cells])

    @pl.loop(0, share // 2)
    def _(pair):
        correct(2 * pair)
        correct(2 * pair + 1)

    for j in range(1, tiles):
        copy = remote(
            out8.at[others[j]],
            in8.at[part(tile)],
            back_send.at[j, 0],
            back_recv.at[tile, 0],
            {"tile": others[j]},
        )
        copy.start()
        sent.append(copy)
    for j in [*range(1, tiles), 0]:
        copy = remote(
            out4.at[others[j]],
            in4.at[part(tile)],
            back_send.at[j, 1],
            back_recv.at[tile, 1],
            {"tile": others[j], "plane": other},
        )
        copy.start()
        sent.append(copy)
    keep = pltpu.make_async_copy(out8.at[tile], in8.at[part(tile)], local_sem.at[5])
    keep.start()

    half_copy.wait()
    beside_copy.wait_recv()
    sign = (1 - 2 * plane).astype(jnp.float32)
    axial_m = [
        [0.5 * sign * flux_m[0, u, w] for w in range(variables)] for u in range(variables)
    ]

    @pl.loop(0, steps)
    def _(t):
        slope, rest = [], []
        for v in range(variables):
            layer = beside[t, v]
            face = jnp.concatenate([halves[0, t, v], halves[1, t, v]], axis=0)
            slope.append(layer - face)
            rest.append(-DISSIPATION * (layer + face))
        for u in range(variables):
            total = rest[u]
            for w in range(variables):
                total = total + axial_m[u][w] * slope[w]
            residual[t, u] = residual[t, u] + inv_volume * total

    mixed_m = []
    for u in range(variables):
        line = []
        for i in range(NI):
            total = -DISSIPATION * right_m[u, i]
            for w in range(variables):
                total = total - axial_m[u][w] * right_m[w, i]
            line.append(total)
        mixed_m.append(line)

    face_copy.wait()
    keep.wait()
    for j in range(tiles):
        if j:
            remote(
                out8.at[others[j]],
                in8.at[part(others[j])],
                back_send.at[j, 0],
                back_recv.at[others[j], 0],
                {"tile": others[j]},
            ).wait_recv()
        remote(
            out4.at[others[j]],
            in4.at[part(others[j])],
            back_send.at[j, 1],
            back_recv.at[others[j], 1],
            {"tile": others[j], "plane": other},
        ).wait_recv()

    @pl.loop(0, steps)
    def _(t):
        near = [in8[t, i] for i in range(NI)]
        mine = [jnp.where(plane == 0, x[:face_cells], x[face_cells:]) for x in near]
        far = [in4[t, i] for i in range(NI)]
        for u in range(variables):
            total = mixed_m[u][0] * near[0]
            a = faces[t, plane, u] + right_m[u, 0] * mine[0]
            b = faces[t, other, u] + right_m[u, 0] * far[0]
            for i in range(1, NI):
                total = total + mixed_m[u][i] * near[i]
                a = a + right_m[u, i] * mine[i]
                b = b + right_m[u, i] * far[i]
            residual[t, u] = residual[t, u] + inv_volume * total
            corrected[t, plane, u] = a
            corrected[t, other, u] = b

    for _, swap in swaps:
        swap.wait_send()
    for copy in [*sent, twin_copy, up, down, beside_copy]:
        copy.wait_send()


def fast(
    state,
    boundary,
    inv_volume,
    flux_matrix,
    left_vectors,
    right_vectors,
    gain,
    harmonic_index,
    mode_count,
):
    tiles = lax.axis_size("tile")
    steps, variables, _, cells, stations = state.shape
    face_cells = boundary.shape[3]
    period = cells * tiles
    modes = gain.shape[2]
    share = steps // tiles
    columns = gain.transpose(0, 2, 1, 3, 4).reshape(gain.shape[0], modes, -1)
    offset = jnp.arange(3 * steps, dtype=jnp.int32) + steps
    product = offset[:, None] * harmonic_index[None, :] % (2 * steps)
    waves = jnp.sin(product.astype(jnp.float32) * (math.pi / steps))
    taps = jnp.sum(waves * harmonic_index.astype(jnp.float32)[None, :], axis=1) * (
        OMEGA_SCALE / steps
    )
    turns = np.outer(np.arange(period), np.arange(period)) % period * (2.0 * math.pi / period)
    analysis = np.concatenate([np.cos(turns), np.sin(turns)], axis=0) * (2.0 / period)
    synthesis = np.concatenate([np.cos(turns), np.sin(turns)], axis=1)
    vmem = pl.BlockSpec(memory_space=pltpu.VMEM)
    smem = pl.BlockSpec(memory_space=pltpu.SMEM)
    anywhere = pl.BlockSpec(memory_space=pl.ANY)
    sizes = (tiles, steps, variables, cells, face_cells, modes, period)
    f32 = jnp.float32
    dma = pltpu.SemaphoreType.DMA
    flat = (steps, variables, cells, stations)
    residual, corrected = pl.pallas_call(
        functools.partial(fast_kernel, sizes),
        out_shape=(
            jax.ShapeDtypeStruct(flat, f32),
            jax.ShapeDtypeStruct(boundary.shape, f32),
        ),
        in_specs=[anywhere, anywhere, vmem, smem, smem, smem, vmem, vmem, smem, vmem, vmem],
        out_specs=(vmem, vmem),
        scratch_shapes=[
            pltpu.VMEM(flat, f32),
            pltpu.VMEM(flat, f32),
            pltpu.VMEM(flat, f32),
            pltpu.VMEM(boundary.shape, f32),
            pltpu.VMEM((2, steps, variables, face_cells, stations), f32),
            pltpu.VMEM((tiles, 2, share, variables, face_cells, stations), f32),
            pltpu.VMEM((tiles, share, NI, cells, stations), f32),
            pltpu.VMEM((tiles, share, NI, face_cells, stations), f32),
            pltpu.VMEM((steps, NI, cells, stations), f32),
            pltpu.VMEM((steps, NI, face_cells, stations), f32),
            pltpu.VMEM((2, variables, steps, stations), f32),
            pltpu.VMEM((variables, steps, stations), f32),
            pltpu.VMEM((variables, steps, stations), f32),
            pltpu.VMEM((3 * steps, cells, stations), f32),
            pltpu.VMEM((columns.shape[2], period, stations), f32),
            pltpu.VMEM((period, stations), f32),
            dma((6,)),
            dma((tiles,)),
            dma((tiles,)),
            dma((tiles, 2)),
            dma((tiles, 2)),
            dma((tiles, 2)),
            dma((tiles, 2)),
            dma((4,)),
            dma((4,)),
        ],
        compiler_params=pltpu.CompilerParams(
            collective_id=0, has_side_effects=True, vmem_limit_bytes=32 * 1024 * 1024
        ),
        name="residual_kernel",
    )(
        state.reshape(flat),
        boundary,
        inv_volume,
        flux_matrix,
        left_vectors,
        right_vectors,
        columns,
        mode_count,
        taps,
        jnp.asarray(analysis, f32),
        jnp.asarray(synthesis, f32),
    )
    return (residual.reshape(state.shape), corrected)


def either(mesh):
    tiles, planes, insts = (mesh.shape[name] for name in ("tile", "plane", "inst"))

    def run(*args):
        state, boundary, gain = (args[0], args[1], args[6])
        steps, _, layers, cells, stations = state.shape
        modes, period = (gain.shape[2], cells * tiles)
        suits = (
            planes == boundary.shape[1] == 2
            and insts == 2
            and tiles > 2
            and steps % (2 * tiles) == 0
            and steps % 8 == 0
            and layers == 1
            and cells == 8
            and cells == 2 * boundary.shape[3]
            and stations % 128 == 0
            and modes % period == 0
        )
        return (fast if suits else local)(*args)

    return run


def solution(mesh):
    return jax.shard_map(
        either(mesh),
        mesh=mesh,
        in_specs=(
            P("inst", "groups", "plane", "tile", None),
            P("inst", None, "groups", ("tile", "plane"), None),
            P(("groups", "plane"), "tile", None),
            P("groups", None, None),
            P("groups", None),
            P("groups", None),
            P("groups", None, None, None, None),
            P("groups"),
            P("groups", None),
        ),
        out_specs=(
            P("inst", "groups", "plane", "tile", None),
            P("inst", None, "groups", ("tile", "plane"), None),
        ),
        check_vma=False,
    )
```

```python
import functools
import math

import jax
import jax.numpy as jnp
import numpy as np
from jax import lax
from jax.experimental import pallas as pl
from jax.experimental.pallas import tpu as pltpu
from jax.sharding import PartitionSpec as P

NI = 2


precise = lax.Precision.HIGHEST
DISSIPATION = 0.25
OMEGA_SCALE = 0.1


def padded_2(x, sides, width):
    for axis, dim in sides:
        size, length = (lax.axis_size(axis), x.shape[dim])
        up = [(i, (i + 1) % size) for i in range(size)]
        down = [(j, i) for i, j in up]
        last = lax.slice_in_dim(x, length - width, length, axis=dim)
        initial = lax.slice_in_dim(x, 0, width, axis=dim)
        before = lax.ppermute(last, axis, up)
        after = lax.ppermute(initial, axis, down)
        x = jnp.concatenate([before, x, after], axis=dim)
    return x


def cell_tables(cell_ids, mode_total, period):
    product = cell_ids[:, None] * jnp.arange(mode_total, dtype=jnp.int32)[None, :] % period
    phases = product.astype(jnp.float32) * (2.0 * math.pi / period)
    return (jnp.cos(phases), jnp.sin(phases))


def time_tables(harmonic_index, instance_ids, period):
    product = instance_ids[:, None] * harmonic_index[None, :] % period
    phases = product.astype(jnp.float32) * (2.0 * math.pi / period)
    cos_table = jnp.cos(phases)
    sin_table = jnp.sin(phases)
    frequency = harmonic_index.astype(jnp.float32)[None, :]
    analysis = jnp.concatenate([cos_table, sin_table], axis=1).T * (2.0 / period)
    synthesis = (
        jnp.concatenate([-frequency * sin_table, frequency * cos_table], axis=1) * OMEGA_SCALE
    )
    return (analysis, synthesis)


def correct_block(block, cell_ids, period, left_vectors, right_vectors, gain, resolved):
    mode_total = gain.shape[2]
    cos_table, sin_table = cell_tables(cell_ids, mode_total, period)
    both_tables = jnp.concatenate([cos_table, sin_table], axis=1)
    spectrum = jnp.einsum("tpvcr,cm->tpvmr", block, both_tables * (2.0 / period), precision=precise)
    hat_cos = spectrum[:, :, :, :mode_total]
    hat_sin = spectrum[:, :, :, mode_total:]
    wave_cos = jnp.einsum("uv,tpvmr->tpumr", left_vectors, hat_cos, precision=precise)
    wave_sin = jnp.einsum("uv,tpvmr->tpumr", left_vectors, hat_sin, precision=precise)
    gain_real = gain[:, 0]
    gain_imag = gain[:, 1]
    out_cos = wave_cos[:, :, NI:]
    out_sin = wave_sin[:, :, NI:]
    target_cos = jnp.einsum(
        "pmio,tpomr->tpimr", gain_real, out_cos, precision=precise
    ) - jnp.einsum("pmio,tpomr->tpimr", gain_imag, out_sin, precision=precise)
    target_sin = jnp.einsum(
        "pmio,tpomr->tpimr", gain_imag, out_cos, precision=precise
    ) + jnp.einsum("pmio,tpomr->tpimr", gain_real, out_sin, precision=precise)
    jump_cos = (target_cos - wave_cos[:, :, :NI]) * resolved[None, :, None]
    jump_sin = (target_sin - wave_sin[:, :, :NI]) * resolved[None, :, None]
    back_cos = jnp.einsum("ui,tpimr->tpumr", right_vectors[:, :NI], jump_cos, precision=precise)
    back_sin = jnp.einsum("ui,tpimr->tpumr", right_vectors[:, :NI], jump_sin, precision=precise)
    joined = jnp.concatenate([back_cos, back_sin], axis=3)
    delta = jnp.einsum("tpumr,cm->tpucr", joined, both_tables, precision=precise)
    return block + delta


def local(
    state,
    boundary,
    inv_volume,
    flux_matrix,
    left_vectors,
    right_vectors,
    gain,
    harmonic_index,
    mode_count,
):
    tiles = lax.axis_size("tile")
    planes = lax.axis_size("plane")
    face_cells = boundary.shape[3]
    period = face_cells * tiles * planes
    local_stations = boundary.shape[4] // (tiles * planes)
    station = lax.axis_index("tile") * planes + lax.axis_index("plane")
    station_modes = lax.dynamic_slice_in_dim(
        mode_count, station * local_stations, local_stations, 1
    )
    resolved = (
        jnp.arange(gain.shape[2], dtype=jnp.int32)[None, :, None] < station_modes[:, None, :]
    ).astype(jnp.float32)
    natural_ids = jnp.arange(period, dtype=jnp.int32)
    fixed = correct_block(
        lax.all_to_all(boundary, ("tile", "plane"), split_axis=4, concat_axis=3, tiled=True),
        natural_ids,
        period,
        left_vectors,
        right_vectors,
        gain,
        resolved,
    )
    corrected = lax.all_to_all(fixed, ("tile", "plane"), split_axis=3, concat_axis=4, tiled=True)
    padded = padded_2(state, (("tile", 3), ("plane", 2)), 1)
    layers = lax.all_gather(corrected, "plane", axis=3, tiled=True)
    plane_pos = lax.axis_index("plane")
    centre = padded[:, :, :, 1:-1]
    inlet_layer = jnp.where(plane_pos == 0, layers[:, 0], centre[:, :, 0])
    exit_layer = jnp.where(plane_pos == planes - 1, layers[:, 1], centre[:, :, -1])
    axial = jnp.concatenate([inlet_layer[:, :, None], state, exit_layer[:, :, None]], axis=2)
    radial = jnp.pad(state, ((0, 0), (0, 0), (0, 0), (0, 0), (1, 1)))
    middle = padded[:, :, 1:-1]
    neighbours = (
        (axial[:, :, 2:], axial[:, :, :-2]),
        (middle[:, :, :, 2:], middle[:, :, :, :-2]),
        (radial[..., 2:], radial[..., :-2]),
    )
    total = jnp.zeros_like(state)
    for direction in range(3):
        forward, backward = neighbours[direction]
        total = total + jnp.einsum(
            "vw,twacr->tvacr", flux_matrix[direction], 0.5 * (forward - backward), precision=precise
        )
        total = total - DISSIPATION * (forward - 2.0 * state + backward)
    flux = inv_volume[None, None] * total
    local_count = state.shape[0]
    total_count = local_count * lax.axis_size("inst")
    instance_ids = lax.axis_index("inst") * local_count + jnp.arange(local_count, dtype=jnp.int32)
    analysis_local, synthesis_local = time_tables(harmonic_index, instance_ids, total_count)
    flat_state = state.reshape(local_count, -1)
    analysis_full, unused_table = time_tables(
        harmonic_index, jnp.arange(total_count, dtype=jnp.int32), total_count
    )
    combined = jnp.dot(synthesis_local, analysis_full, precision=precise)
    rate = jnp.dot(
        combined, lax.all_gather(flat_state, "inst", axis=0, tiled=True), precision=precise
    )
    residual = flux + rate.reshape(state.shape)
    return (residual, corrected)


def fast_kernel(
    sizes,
    state,
    boundary,
    volume,
    flux_m,
    left_m,
    right_m,
    columns,
    counts,
    harmonics,
    analysis,
    synthesis,
    residual,
    corrected,
    own,
    twin,
    beside,
    faces,
    halves,
    spread,
    out8,
    relay,
    in8,
    in4,
    edges,
    below,
    above,
    taps_wide,
    gains,
    resolved,
    local_sem,
    swap_send,
    swap_recv,
    spread_send,
    spread_recv,
    back_send,
    back_recv,
    state_send,
    state_recv,
):
    tiles, steps, variables, cells, face_cells, modes, period = sizes
    share = steps // tiles
    piece = share // 2
    tile = lax.axis_index("tile")
    plane = lax.axis_index("plane")
    inst = lax.axis_index("inst")
    other = 1 - plane
    mesh_id = pl.DeviceIdType.MESH
    others = [lax.rem(tile + j, tiles) for j in range(tiles)]

    own_copy = pltpu.make_async_copy(state, own, local_sem.at[0])
    own_copy.start()
    face_copy = pltpu.make_async_copy(boundary, faces, local_sem.at[1])
    face_copy.start()
    half_copy = pltpu.make_async_copy(boundary.at[:, plane], halves.at[plane], local_sem.at[2])
    half_copy.start()

    barrier = pltpu.get_barrier_semaphore()
    for j in range(1, tiles):
        pl.semaphore_signal(
            barrier, inc=1, device_id={"tile": others[j]}, device_id_type=mesh_id
        )
    pl.semaphore_signal(barrier, inc=1, device_id={"plane": other}, device_id_type=mesh_id)
    pl.semaphore_signal(barrier, inc=1, device_id={"inst": 1 - inst}, device_id_type=mesh_id)
    pl.semaphore_wait(barrier, tiles + 1)

    def remote(src, dst, send, recv, where):
        return pltpu.make_async_remote_copy(
            src_ref=src,
            dst_ref=dst,
            send_sem=send,
            recv_sem=recv,
            device_id=where,
            device_id_type=mesh_id,
        )

    def part(k, h):
        return pl.ds(k * share + h * piece, piece)

    def whole(k):
        return pl.ds(k * share, share)

    order = [(j, h) for h in range(2) for j in [*range(1, tiles), 0]]
    swaps = []
    for j, h in order:
        swap = remote(
            boundary.at[part(others[j], h), other],
            halves.at[plane, part(others[j], h)],
            swap_send.at[j, h],
            swap_recv.at[j, h],
            {"plane": other},
        )
        swap.start()
        swaps.append((j, h, swap))
    sent = []
    for j, h in order:
        if j:
            copy = remote(
                boundary.at[part(others[j], h), plane],
                spread.at[tile, plane, h * piece : (h + 1) * piece],
                spread_send.at[j, 0, h],
                spread_recv.at[tile, plane, h],
                {"tile": others[j]},
            )
            copy.start()
            sent.append(copy)
    twin_copy = remote(state, twin, state_send.at[0], state_recv.at[0], {"inst": 1 - inst})
    twin_copy.start()
    home = pltpu.make_async_copy(
        boundary.at[whole(tile), plane], spread.at[tile, plane], local_sem.at[3]
    )
    home.start()

    own_copy.wait()

    @pl.loop(0, steps)
    def _(t):
        for v in range(variables):
            edges[0, v, pl.ds(t, 1), :] = own[t, v, cells - 1 : cells, :]
            edges[1, v, pl.ds(t, 1), :] = own[t, v, 0:1, :]

    up = remote(
        edges.at[0], below, state_send.at[1], state_recv.at[1], {"tile": others[1]}
    )
    up.start()
    down = remote(
        edges.at[1], above, state_send.at[2], state_recv.at[2], {"tile": others[tiles - 1]}
    )
    down.start()

    beside_copy = remote(state, beside, state_send.at[3], state_recv.at[3], {"plane": other})
    for place, (j, h, swap) in enumerate(swaps):
        if place == len(swaps) - 1:
            beside_copy.start()
        swap.wait_recv()
        if j:
            copy = remote(
                halves.at[other, part(others[j], h)],
                spread.at[tile, other, h * piece : (h + 1) * piece],
                spread_send.at[j, 1, h],
                spread_recv.at[tile, other, h],
                {"tile": others[j]},
            )
            copy.start()
            sent.append(copy)
    away = pltpu.make_async_copy(
        halves.at[other, whole(tile)], spread.at[tile, other], local_sem.at[4]
    )
    away.start()

    count_row = jnp.where(plane == 0, counts[0:1, :], counts[1:2, :])
    stations = counts.shape[1]
    mode_row = lax.broadcasted_iota(jnp.int32, (period, stations), 0)
    mask = [
        (mode_row + a * period < count_row).astype(jnp.float32) for a in range(modes // period)
    ]
    resolved[...] = sum(mask[1:], mask[0])
    for k in range(gains.shape[0]):
        total = None
        for a in range(modes // period):
            column = columns[plane, a * period : (a + 1) * period, k : k + 1]
            term = mask[a] * jnp.broadcast_to(column, (period, stations))
            total = term if total is None else total + term
        gains[k] = total

    number = harmonics.shape[0]
    padded = -(-number // 8) * 8
    depth = lax.broadcasted_iota(jnp.int32, (padded, stations), 0)
    distance = lax.broadcasted_iota(jnp.int32, (padded, stations), 1).astype(jnp.float32) + steps
    frequency = jnp.zeros((padded, stations), jnp.float32)
    for k in range(number):
        frequency = jnp.where(depth == k, harmonics[k].astype(jnp.float32), frequency)
    turn = frequency * distance
    turn = turn - 2.0 * steps * jnp.floor((turn + 0.5) * (0.5 / steps))
    turn = jnp.where(turn > steps, turn - 2.0 * steps, turn)
    turn = jnp.where(turn > 0.5 * steps, steps - turn, turn)
    turn = jnp.where(turn < -0.5 * steps, -steps - turn, turn)
    angle = turn * (math.pi / steps)
    square = angle * angle
    series = jnp.full((padded, stations), -1.0 / math.factorial(15), jnp.float32)
    for n in range(13, 0, -2):
        series = series * square + (1.0 if n % 4 == 1 else -1.0) / math.factorial(n)
    weights = jnp.sum(frequency * angle * series, axis=0, keepdims=True) * (OMEGA_SCALE / steps)
    weights = jnp.broadcast_to(weights, (cells, stations))
    for e in range(3 * steps):
        taps_wide[e] = jnp.broadcast_to(weights[:, e : e + 1], (cells, stations))

    twin_copy.wait_recv()

    @pl.loop(0, variables)
    def _(v):
        @pl.loop(0, steps // 8)
        def _(block):
            base = steps - 8 * block
            held = {}

            def tap(offset):
                if offset not in held:
                    held[offset] = taps_wide[base + offset]
                return held[offset]

            sums = [None] * 8
            for source, shift in ((own, 0), (twin, steps)):
                for j in range(steps):
                    x = source[j, v]
                    for i in range(8):
                        term = tap(j - i + shift) * x
                        sums[i] = term if sums[i] is None else sums[i] + term
            for i in range(8):
                residual[8 * block + i, v] = sums[i]

    up.wait_recv()
    down.wait_recv()
    inv_volume = volume[0]
    row = lax.broadcasted_iota(jnp.int32, (cells, stations), 0)
    lane = lax.broadcasted_iota(jnp.int32, (cells, stations), 1)

    @pl.loop(0, steps)
    def _(t):
        around, across, rest = [], [], []
        for v in range(variables):
            s = own[t, v]
            ahead = jnp.where(
                row == cells - 1, above[v, pl.ds(t, 1), :], pltpu.roll(s, cells - 1, 0)
            )
            behind = jnp.where(row == 0, below[v, pl.ds(t, 1), :], pltpu.roll(s, 1, 0))
            outer = jnp.where(lane == stations - 1, 0.0, pltpu.roll(s, stations - 1, 1))
            inner = jnp.where(lane == 0, 0.0, pltpu.roll(s, 1, 1))
            around.append(0.5 * (ahead - behind))
            across.append(0.5 * (outer - inner))
            rest.append(DISSIPATION * (6.0 * s - (ahead + behind + outer + inner)))
        for u in range(variables):
            total = rest[u]
            for w in range(variables):
                total = total + flux_m[1, u, w] * around[w]
                total = total + flux_m[2, u, w] * across[w]
            residual[t, u] = residual[t, u] + inv_volume * total

    def correct(t):
        x = [
            jnp.concatenate(
                [spread[k, h, t, v] for k in range(tiles) for h in range(2)], axis=0
            )
            for v in range(variables)
        ]
        mixed = []
        for u in range(variables):
            total = left_m[u, 0] * x[0]
            for v in range(1, variables):
                total = total + left_m[u, v] * x[v]
            mixed.append(total)
        waves = jnp.dot(
            analysis[...],
            jnp.concatenate(mixed, axis=1),
            precision=precise,
            preferred_element_type=jnp.float32,
        )
        part_cos = [waves[:period, u * stations : (u + 1) * stations] for u in range(variables)]
        part_sin = [waves[period:, u * stations : (u + 1) * stations] for u in range(variables)]
        jumps = []
        outgoing = variables - NI
        for i in range(NI):
            jump_cos = -resolved[...] * part_cos[i]
            jump_sin = -resolved[...] * part_sin[i]
            for o in range(outgoing):
                real = gains[i * outgoing + o]
                imag = gains[(NI + i) * outgoing + o]
                jump_cos = jump_cos + real * part_cos[NI + o] - imag * part_sin[NI + o]
                jump_sin = jump_sin + imag * part_cos[NI + o] + real * part_sin[NI + o]
            jumps.append(jnp.concatenate([jump_cos, jump_sin], axis=0))
        delta = jnp.dot(
            synthesis[...],
            jnp.concatenate(jumps, axis=1),
            precision=precise,
            preferred_element_type=jnp.float32,
        )
        for k in range(tiles):
            for i in range(NI):
                block = delta[k * cells : (k + 1) * cells, i * stations : (i + 1) * stations]
                out8[k, t, i] = block

    home.wait()
    away.wait()
    keeps = []
    for h in range(2):
        for j in range(1, tiles):
            for side in range(2):
                span = spread.at[others[j], side, h * piece : (h + 1) * piece]
                remote(
                    span,
                    span,
                    spread_send.at[j, side, h],
                    spread_recv.at[others[j], side, h],
                    {"tile": others[j]},
                ).wait_recv()
        for t in range(piece):
            correct(h * piece + t)
        for j in range(1, tiles):
            copy = remote(
                out8.at[others[j], h * piece : (h + 1) * piece],
                in8.at[part(tile, h)],
                back_send.at[j, 0, h],
                back_recv.at[tile, 0, h],
                {"tile": others[j]},
            )
            copy.start()
            sent.append(copy)
        keep = pltpu.make_async_copy(
            out8.at[tile, h * piece : (h + 1) * piece],
            in8.at[part(tile, h)],
            local_sem.at[5 + h],
        )
        keep.start()
        keeps.append(keep)

    half_copy.wait()
    for h in range(2):
        for j in range(tiles):
            source = others[j]
            if j:
                remote(
                    out8.at[source, h * piece : (h + 1) * piece],
                    in8.at[part(source, h)],
                    back_send.at[j, 0, h],
                    back_recv.at[source, 0, h],
                    {"tile": source},
                ).wait_recv()
            else:
                keeps[h].wait()
            first = source * share + h * piece
            for t in range(piece):
                for i in range(NI):
                    block = in8[first + t, i]
                    relay[first + t, i] = jnp.where(
                        plane == 0, block[face_cells:], block[:face_cells]
                    )
            copy = remote(
                relay.at[part(source, h)],
                in4.at[part(source, h)],
                back_send.at[j, 1, h],
                back_recv.at[j, 1, h],
                {"plane": other},
            )
            copy.start()
            sent.append(copy)

    beside_copy.wait_recv()
    sign = (1 - 2 * plane).astype(jnp.float32)
    axial_m = [
        [0.5 * sign * flux_m[0, u, w] for w in range(variables)] for u in range(variables)
    ]

    @pl.loop(0, steps)
    def _(t):
        slope, rest = [], []
        for v in range(variables):
            layer = beside[t, v]
            face = jnp.concatenate([halves[0, t, v], halves[1, t, v]], axis=0)
            slope.append(layer - face)
            rest.append(-DISSIPATION * (layer + face))
        for u in range(variables):
            total = rest[u]
            for w in range(variables):
                total = total + axial_m[u][w] * slope[w]
            residual[t, u] = residual[t, u] + inv_volume * total

    mixed_m = []
    for u in range(variables):
        line = []
        for i in range(NI):
            total = -DISSIPATION * right_m[u, i]
            for w in range(variables):
                total = total - axial_m[u][w] * right_m[w, i]
            line.append(total)
        mixed_m.append(line)

    face_copy.wait()
    for h in range(2):
        for j in range(tiles):
            remote(
                relay.at[part(others[j], h)],
                in4.at[part(others[j], h)],
                back_send.at[j, 1, h],
                back_recv.at[j, 1, h],
                {"plane": other},
            ).wait_recv()

    @pl.loop(0, steps)
    def _(t):
        near = [in8[t, i] for i in range(NI)]
        mine = [jnp.where(plane == 0, x[:face_cells], x[face_cells:]) for x in near]
        far = [in4[t, i] for i in range(NI)]
        for u in range(variables):
            total = mixed_m[u][0] * near[0]
            a = faces[t, plane, u] + right_m[u, 0] * mine[0]
            b = faces[t, other, u] + right_m[u, 0] * far[0]
            for i in range(1, NI):
                total = total + mixed_m[u][i] * near[i]
                a = a + right_m[u, i] * mine[i]
                b = b + right_m[u, i] * far[i]
            residual[t, u] = residual[t, u] + inv_volume * total
            corrected[t, plane, u] = a
            corrected[t, other, u] = b

    for _, _, swap in swaps:
        swap.wait_send()
    for copy in [*sent, twin_copy, up, down, beside_copy]:
        copy.wait_send()


def fast(
    state,
    boundary,
    inv_volume,
    flux_matrix,
    left_vectors,
    right_vectors,
    gain,
    harmonic_index,
    mode_count,
):
    tiles = lax.axis_size("tile")
    steps, variables, _, cells, stations = state.shape
    face_cells = boundary.shape[3]
    period = cells * tiles
    modes = gain.shape[2]
    share = steps // tiles
    columns = gain.transpose(0, 2, 1, 3, 4).reshape(gain.shape[0], modes, -1)
    turns = np.outer(np.arange(period), np.arange(period)) % period * (2.0 * math.pi / period)
    analysis = np.concatenate([np.cos(turns), np.sin(turns)], axis=0) * (2.0 / period)
    synthesis = np.concatenate([np.cos(turns), np.sin(turns)], axis=1)
    vmem = pl.BlockSpec(memory_space=pltpu.VMEM)
    smem = pl.BlockSpec(memory_space=pltpu.SMEM)
    anywhere = pl.BlockSpec(memory_space=pl.ANY)
    sizes = (tiles, steps, variables, cells, face_cells, modes, period)
    f32 = jnp.float32
    dma = pltpu.SemaphoreType.DMA
    flat = (steps, variables, cells, stations)
    residual, corrected = pl.pallas_call(
        functools.partial(fast_kernel, sizes),
        out_shape=(
            jax.ShapeDtypeStruct(flat, f32),
            jax.ShapeDtypeStruct(boundary.shape, f32),
        ),
        in_specs=[anywhere, anywhere, vmem, smem, smem, smem, vmem, vmem, smem, vmem, vmem],
        out_specs=(vmem, vmem),
        scratch_shapes=[
            pltpu.VMEM(flat, f32),
            pltpu.VMEM(flat, f32),
            pltpu.VMEM(flat, f32),
            pltpu.VMEM(boundary.shape, f32),
            pltpu.VMEM((2, steps, variables, face_cells, stations), f32),
            pltpu.VMEM((tiles, 2, share, variables, face_cells, stations), f32),
            pltpu.VMEM((tiles, share, NI, cells, stations), f32),
            pltpu.VMEM((steps, NI, face_cells, stations), f32),
            pltpu.VMEM((steps, NI, cells, stations), f32),
            pltpu.VMEM((steps, NI, face_cells, stations), f32),
            pltpu.VMEM((2, variables, steps, stations), f32),
            pltpu.VMEM((variables, steps, stations), f32),
            pltpu.VMEM((variables, steps, stations), f32),
            pltpu.VMEM((3 * steps, cells, stations), f32),
            pltpu.VMEM((columns.shape[2], period, stations), f32),
            pltpu.VMEM((period, stations), f32),
            dma((7,)),
            dma((tiles, 2)),
            dma((tiles, 2)),
            dma((tiles, 2, 2)),
            dma((tiles, 2, 2)),
            dma((tiles, 2, 2)),
            dma((tiles, 2, 2)),
            dma((4,)),
            dma((4,)),
        ],
        compiler_params=pltpu.CompilerParams(
            collective_id=0, has_side_effects=True, vmem_limit_bytes=32 * 1024 * 1024
        ),
        name="residual_kernel",
    )(
        state.reshape(flat),
        boundary,
        inv_volume,
        flux_matrix,
        left_vectors,
        right_vectors,
        columns,
        mode_count,
        harmonic_index,
        jnp.asarray(analysis, f32),
        jnp.asarray(synthesis, f32),
    )
    return (residual.reshape(state.shape), corrected)


def either(mesh):
    tiles, planes, insts = (mesh.shape[name] for name in ("tile", "plane", "inst"))

    def run(*args):
        state, boundary, gain = (args[0], args[1], args[6])
        steps, _, layers, cells, stations = state.shape
        modes, period = (gain.shape[2], cells * tiles)
        suits = (
            planes == boundary.shape[1] == 2
            and insts == 2
            and tiles > 2
            and steps % (2 * tiles) == 0
            and steps % 8 == 0
            and layers == 1
            and cells == 8
            and cells == 2 * boundary.shape[3]
            and stations % 128 == 0
            and 3 * steps <= stations
            and modes % period == 0
        )
        return (fast if suits else local)(*args)

    return run


def solution(mesh):
    return jax.shard_map(
        either(mesh),
        mesh=mesh,
        in_specs=(
            P("inst", "groups", "plane", "tile", None),
            P("inst", None, "groups", ("tile", "plane"), None),
            P(("groups", "plane"), "tile", None),
            P("groups", None, None),
            P("groups", None),
            P("groups", None),
            P("groups", None, None, None, None),
            P("groups"),
            P("groups", None),
        ),
        out_specs=(
            P("inst", "groups", "plane", "tile", None),
            P("inst", None, "groups", ("tile", "plane"), None),
        ),
        check_vma=False,
    )
```
